1024 devices in a mesh: rep: 32 (over x_hi, z), fsdp: 32 (over x_lo, y, core).
Axes of the slice: x: 8 (x_hi: 4, x_lo: 2; x = x_hi * 2 + x_lo), y: 8, z: 8, core: 2. Of those that a mesh axis runs over, the one named last changes fastest.
Arguments:
- acts: bfloat16 [32, 8192, 2048], P('rep', 'fsdp'), may hold values from -6 to 6
- grad_out: bfloat16 [32, 8192, 1024], P('rep', 'fsdp'), may hold values from -0.13258252 to 0.13258252
- inner_weight: float32 [32, 2048, 1024], P('rep', 'fsdp'), may hold values from -0.03 to 0.03
- first_moment: float32 [32, 2048, 1024], P('rep', 'fsdp'), may hold values from -6 to 6
- second_moment: float32 [32, 2048, 1024], P('rep', 'fsdp'), may hold values from 0.1 to 10
- outer_weight: float32 [2048, 1024], P(('fsdp', 'rep')), may hold values from -0.03 to 0.03
- outer_momentum: float32 [2048, 1024], P(('fsdp', 'rep')), may hold values from -0.0006 to 0.0006
Outputs:
- outer_next: float32 [2048, 1024], P(('fsdp', 'rep'))
- momentum_next: float32 [2048, 1024], P(('fsdp', 'rep'))
- weight_next: bfloat16 [2048, 1024], P('fsdp')
The draws below stay inside these ranges and needn't reach their ends.
All inputs are finite; a program needn't handle non-finite values.
Results may differ from the reference program's by a relative error of at most 0.008.
Values may be sent and summed in bfloat16 or wider, within the bound.
No kernel may reach another device: no remote copies, remote signals or barrier semaphores. Data moves between devices by JAX's collectives and lax.ppermute only.
A program may use at most 32 MiB of HBM per device.

```python
import math
import jax
import jax.numpy as jnp
from jax import lax

D = 2048
KVW = 1024
TOK_DEV = 256
INNER_STEP = 500
REPLICAS = 32
TOKENS = 8192
N_FSDP = 32


def shared_weight(key):
    return jnp.clip(jax.random.normal(key, (D, KVW), jnp.float32), -6.0, 6.0) * (0.1 * D ** (-0.5))


def draw_outer_weight(key, part):
    common = shared_weight(key)
    return common


def draw_inner_weight(key, part):
    common = shared_weight(key)
    key = jax.random.fold_in(key, 2)
    key_common, key_own = jax.random.split(key)
    together = jnp.clip(jax.random.normal(key_common, (D, KVW), jnp.float32), -4.0, 4.0) * 0.0001
    apart = jnp.clip(jax.random.normal(key_own, (REPLICAS, D, KVW), jnp.float32), -4.0, 4.0) * 0.0003
    return common[None] + together[None] + apart


def draw_acts(key, part):
    key = jax.random.fold_in(key, 3)
    key_common, key_own = jax.random.split(key)
    shared = jax.random.normal(key_common, (TOKENS, D), jnp.float32)
    own = jax.random.normal(key_own, (REPLICAS, TOKENS, D), jnp.float32)
    mixed = 0.8944272 * shared[None] + 0.4472136 * own
    return jnp.clip(mixed, -6.0, 6.0).astype(jnp.bfloat16)


def draw_grad_out(key, part):
    key = jax.random.fold_in(key, 4)
    key_common, key_own = jax.random.split(key)
    shared = jax.random.normal(key_common, (TOKENS, KVW), jnp.float32)
    own = jax.random.normal(key_own, (REPLICAS, TOKENS, KVW), jnp.float32)
    mixed = 0.8944272 * shared[None] + 0.4472136 * own
    return (jnp.clip(mixed, -6.0, 6.0) * (2.0 * TOKENS ** (-0.5))).astype(jnp.bfloat16)


def shard_levels(rng, extent, cuts, low, largest):
    gain = 1.0
    for axis_at, parts in cuts:
        steps = jax.random.uniform(jax.random.fold_in(jax.random.fold_in(rng, 6), axis_at), (parts,), jnp.float32, low / len(cuts), largest / len(cuts))
        gain = gain * jnp.repeat(jnp.exp(steps), extent[axis_at] // parts).reshape((-1,) + (1,) * (len(extent) - 1 - axis_at))
    return gain


def centred(rng, shape, spread, most, pieces=(), held_as=jnp.bfloat16):
    drawn = spread * jax.random.normal(rng, shape, jnp.float32)
    if pieces:
        drawn = drawn * shard_levels(rng, shape, pieces, -0.22, 0.18)
    return jnp.clip(drawn, -most, most).astype(held_as)


def setup_inputs(seed: int = 0) -> dict:
    splits = jax.random.split(jax.random.key(seed), 8)
    return {
        "acts": draw_acts(jax.random.fold_in(splits[7], 71), 0),
        "grad_out": draw_grad_out(jax.random.fold_in(splits[7], 71), 0),
        "inner_weight": draw_inner_weight(jax.random.fold_in(splits[7], 71), 0),
        "first_moment": centred(splits[3], (REPLICAS, D, KVW), 1.0, 6.0, ((0, 32), (1, 32)), jnp.float32),
        "second_moment": jnp.clip(jnp.exp(math.log(10.0) - 4.6051702 * jax.random.uniform(splits[4], (REPLICAS, D, KVW), jnp.float32) ** shard_levels(splits[4], (REPLICAS, D, KVW), ((0, 32), (1, 32)), -0.2, 0.2)), 0.1, 10.0),
        "outer_weight": draw_outer_weight(jax.random.fold_in(splits[7], 71), 0),
        "outer_momentum": centred(splits[6], (D, KVW), 0.0001, 0.0006, ((0, 1024),), jnp.float32),
    }


def replica_step(acts, grad_out, inner_weight, first_moment, second_moment):
    blocks = acts.reshape(N_FSDP, TOK_DEV, D)
    cotangents = grad_out.reshape(N_FSDP, TOK_DEV, KVW)

    def add_block(total, pair):
        partial_sum = jnp.dot(pair[0].T, pair[1], preferred_element_type=jnp.float32).astype(jnp.bfloat16)
        return (total + partial_sum.astype(jnp.float32), None)
    grad, unused = lax.scan(add_block, jnp.zeros((D, KVW), jnp.float32), (blocks, cotangents))
    first = 0.9 * first_moment + 0.1 * grad
    second = 0.95 * second_moment + 0.05 * grad * grad
    first_hat = first / (1.0 - 0.9 ** INNER_STEP)
    second_hat = second / (1.0 - 0.95 ** INNER_STEP)
    updated = inner_weight * (1.0 - 0.0004 * 0.1) - 0.0004 * first_hat / (jnp.sqrt(second_hat) + 1e-08)
    return updated

def reference(acts, grad_out, inner_weight, first_moment, second_moment, outer_weight, outer_momentum):

    def add_replica(total, items):
        inner_new = replica_step(*items)
        return (total + inner_new, None)
    summed, unused = lax.scan(add_replica, jnp.zeros((D, KVW), jnp.float32), (acts, grad_out, inner_weight, first_moment, second_moment))
    pseudo = outer_weight - summed / REPLICAS
    momentum_next = 0.9 * outer_momentum + pseudo
    outer_next = outer_weight - 0.7 * (pseudo + 0.9 * momentum_next)
    return (outer_next, momentum_next, outer_next.astype(jnp.bfloat16))
```

```python
import jax
import jax.numpy as jnp
from jax import lax
from jax.sharding import Mesh, PartitionSpec as P

INNER_STEP = 500
AXES = ("xh", "z", "xl", "y", "core")
SIZES = (4, 8, 2, 8, 2)
REP = ("xh", "z")
FSDP = ("xl", "y", "core")


def shards(acts, grad_out, inner_weight, first_moment, second_moment, outer_weight, outer_momentum):
    core = lax.axis_index("core")
    chips = lax.axis_size(("xl", "y"))
    replicas = lax.axis_size(REP)
    rows, cols = inner_weight.shape[1:]
    own = rows // replicas

    with jax.named_scope("grad_product"):
        partial = lax.dot_general(
            acts[0], grad_out[0], (((0,), (0,)), ((), ())), preferred_element_type=jnp.float32
        ).astype(jnp.bfloat16).reshape(chips, 2, rows, cols)
    with jax.named_scope("core_sum"):
        keep = lax.dynamic_index_in_dim(partial, core, 1, keepdims=False)
        give = lax.dynamic_index_in_dim(partial, 1 - core, 1, keepdims=False)
        got = lax.ppermute(give, "core", [(0, 1), (1, 0)])
        chip_sum = (keep.astype(jnp.float32) + got.astype(jnp.float32)).astype(jnp.bfloat16)
    with jax.named_scope("grad_exchange"):
        pieces = lax.all_to_all(chip_sum, ("xl", "y"), 0, 0, tiled=True)
        grad = jnp.sum(pieces.astype(jnp.float32), axis=0)

    with jax.named_scope("adamw"):
        first = 0.9 * first_moment[0] + 0.1 * grad
        second = 0.95 * second_moment[0] + 0.05 * grad * grad
        first_hat = first / (1.0 - 0.9**INNER_STEP)
        second_hat = second / (1.0 - 0.95**INNER_STEP)
        inner_new = inner_weight[0] * (1.0 - 0.0004 * 0.1) - 0.0004 * first_hat / (
            jnp.sqrt(second_hat) + 1e-08
        )
        inner_new = lax.optimization_barrier(inner_new)
    with jax.named_scope("replica_sum"):
        pieces = lax.all_to_all(inner_new.reshape(replicas, own, cols), REP, 0, 0, tiled=True)
        summed = jnp.sum(pieces, axis=0)
    with jax.named_scope("outer_step"):
        pseudo = outer_weight - summed / replicas
        momentum_next = 0.9 * outer_momentum + pseudo
        outer_next = outer_weight - 0.7 * (pseudo + 0.9 * momentum_next)
    with jax.named_scope("row_gather"):
        new = outer_next.astype(jnp.bfloat16).reshape(1, own * cols // 128, 128)
        copies = jnp.broadcast_to(new, (replicas,) + new.shape[1:])
        weight_next = lax.all_to_all(copies, REP, 0, 0, tiled=True).reshape(rows, cols)
    return (outer_next, momentum_next, weight_next)


def solution(mesh, sizes=SIZES):
    grid = Mesh(mesh.devices.reshape(sizes), AXES)
    split = P(REP, FSDP, None)
    outer = P(FSDP + REP, None)
    return jax.shard_map(
        shards,
        mesh=grid,
        in_specs=(split, split, split, split, split, outer, outer),
        out_specs=(outer, outer, P(FSDP, None)),
        check_vma=False,
    )
```

```python
import jax
import jax.numpy as jnp
from jax import lax
from jax.experimental import pallas as pl
from jax.experimental.pallas import tpu as pltpu
from jax.sharding import Mesh, PartitionSpec as P

INNER_STEP = 500
AXES = ("xh", "z", "xl", "y", "core")
SIZES = (4, 8, 2, 8, 2)
REP = ("xh", "z")
FSDP = ("xl", "y", "core")
RING = 8


def product_kernel(offsets, place, acts, cot, acts_peer, cot_peer, *outs):
    xl, y, core = place[0], place[1], place[2]
    lane = lax.broadcasted_iota(jnp.int32, (1, 128), 1)
    own_side = (lane < 64) == (core == 0)

    def columns(ref, target):
        def block(side):
            start = pl.multiple_of((side * RING + target) * 128, 128)
            return ref[:, pl.ds(start, 128)].astype(jnp.float32)

        near, far = block(xl), block(1 - xl)
        still = jnp.where(core == 0, near, far)
        moved = pltpu.roll(jnp.where(core == 0, far, near), 64, 1)
        return jnp.where(own_side, still, moved).astype(jnp.bfloat16)

    def times(lhs, rhs):
        return lax.dot_general(lhs, rhs, (((0,), (0,)), ((), ())), preferred_element_type=jnp.float32)

    for offset, out in zip(offsets, outs):
        target = lax.rem(y + offset, RING)
        total = times(columns(acts, target), cot[...]) + times(columns(acts_peer, target), cot_peer[...])
        out[...] = total.astype(out.dtype)


def product(offsets, place, acts, cot, acts_peer, cot_peer):
    vmem = pl.BlockSpec(memory_space=pltpu.VMEM)
    cols = cot.shape[1]
    tokens = acts.shape[0]
    return pl.pallas_call(
        lambda *refs: product_kernel(offsets, *refs),
        out_shape=[jax.ShapeDtypeStruct((128, cols), jnp.bfloat16) for _ in offsets],
        in_specs=[pl.BlockSpec(memory_space=pltpu.SMEM)] + [vmem] * 4,
        out_specs=[vmem for _ in offsets],
        compiler_params=pltpu.CompilerParams(vmem_limit_bytes=24 * 1024 * 1024),
        cost_estimate=pl.CostEstimate(
            flops=2 * 128 * len(offsets) * 2 * tokens * cols,
            bytes_accessed=4 * tokens * (2048 + cols),
            transcendentals=0,
        ),
    )(place, acts, cot, acts_peer, cot_peer)


def add(*terms):
    return sum(t.astype(jnp.float32) for t in terms)


def shards(acts, grad_out, inner_weight, first_moment, second_moment, outer_weight, outer_momentum):
    replicas = lax.axis_size(REP)
    rows, cols = inner_weight.shape[1:]
    own = rows // replicas
    bf16 = jnp.bfloat16
    place = jnp.stack([lax.axis_index(a) for a in FSDP])

    with jax.named_scope("core_swap"):
        swap = [(0, 1), (1, 0)]
        acts_peer = lax.ppermute(acts[0], "core", swap)
        cot_peer = lax.ppermute(grad_out[0], "core", swap)
    with jax.named_scope("grad_product"):
        four, three, five = product((4, 3, 5), place, acts[0], grad_out[0], acts_peer, cot_peer)
        two, six, one, seven, zero = product((2, 6, 1, 7, 0), place, acts[0], grad_out[0], acts_peer, cot_peer)
    with jax.named_scope("grad_ring"):
        ring = [(i, (i + 1) % RING) for i in range(RING)]
        back = [(j, i) for i, j in ring]
        up = lax.ppermute(four[:rows], "y", ring)
        down = lax.ppermute(four[rows:], "y", back)
        up = jnp.concatenate([add(three[:rows], up).astype(bf16), three[rows:]])
        down = jnp.concatenate([five[:rows], add(five[rows:], down).astype(bf16)])
        for ahead, behind in ((two, six), (one, seven)):
            up = add(ahead, lax.ppermute(up, "y", ring)).astype(bf16)
            down = add(behind, lax.ppermute(down, "y", back)).astype(bf16)
        up = lax.ppermute(up, "y", ring)
        down = lax.ppermute(down, "y", back)
    with jax.named_scope("grad_pair"):
        other = add(zero[rows:], up[rows:], down[rows:]).astype(bf16)
        other = lax.ppermute(other, "xl", [(0, 1), (1, 0)])
        grad = add(zero[:rows], up[:rows], down[:rows], other)

    with jax.named_scope("adamw"):
        first = 0.9 * first_moment[0] + 0.1 * grad
        second = 0.95 * second_moment[0] + 0.05 * grad * grad
        first_hat = first / (1.0 - 0.9**INNER_STEP)
        second_hat = second / (1.0 - 0.95**INNER_STEP)
        inner_new = inner_weight[0] * (1.0 - 0.0004 * 0.1) - 0.0004 * first_hat / (
            jnp.sqrt(second_hat) + 1e-08
        )
        inner_new = lax.optimization_barrier(inner_new)
    with jax.named_scope("replica_sum"):
        pieces = lax.all_to_all(inner_new.reshape(replicas, own, cols), REP, 0, 0, tiled=True)
        summed = jnp.sum(pieces, axis=0)
    with jax.named_scope("outer_step"):
        pseudo = outer_weight - summed / replicas
        momentum_next = 0.9 * outer_momentum + pseudo
        outer_next = outer_weight - 0.7 * (pseudo + 0.9 * momentum_next)
    with jax.named_scope("row_gather"):
        new = outer_next.astype(bf16).reshape(1, own * cols // 128, 128)
        copies = jnp.broadcast_to(new, (replicas,) + new.shape[1:])
        weight_next = lax.all_to_all(copies, REP, 0, 0, tiled=True).reshape(rows, cols)
    return (outer_next, momentum_next, weight_next)


def solution(mesh, sizes=SIZES):
    grid = Mesh(mesh.devices.reshape(sizes), AXES)
    split = P(REP, FSDP, None)
    outer = P(FSDP + REP, None)
    return jax.shard_map(
        shards,
        mesh=grid,
        in_specs=(split, split, split, split, split, outer, outer),
        out_specs=(outer, outer, P(FSDP, None)),
        check_vma=False,
    )
```

```python
import jax
import jax.numpy as jnp
from jax import lax
from jax.experimental import pallas as pl
from jax.experimental.pallas import tpu as pltpu
from jax.sharding import Mesh, PartitionSpec as P

INNER_STEP = 500
AXES = ("xh", "z", "xl", "y", "core")
SIZES = (4, 8, 2, 8, 2)
REP = ("xh", "z")
FSDP = ("xl", "y", "core")
RING = 8
OUTER_GAIN = 0.7 * 1.9


def product_kernel(offsets, place, acts, cot, *refs):
    xl, y, core = place[0], place[1], place[2]
    before, outs = refs[: -len(offsets)], refs[-len(offsets) :]
    lane = lax.broadcasted_iota(jnp.int32, (1, 128), 1)
    own_side = (lane < 64) == (core == 0)

    def columns(target):
        def block(side):
            start = pl.multiple_of((side * RING + target) * 128, 128)
            return acts[:, pl.ds(start, 128)].astype(jnp.float32)

        near, far = block(xl), block(1 - xl)
        still = jnp.where(core == 0, near, far)
        moved = pltpu.roll(jnp.where(core == 0, far, near), 64, 1)
        return jnp.where(own_side, still, moved).astype(jnp.bfloat16)

    for i, offset in enumerate(offsets):
        target = lax.rem(y + jnp.where(core == 0, offset, RING - offset), RING)
        total = lax.dot_general(
            columns(target), cot[...], (((0,), (0,)), ((), ())), preferred_element_type=jnp.float32
        )
        if before:
            total = total + before[i][...]
        outs[i][...] = total.astype(outs[i].dtype)


def product(offsets, dtype, place, acts, cot, *before):
    vmem = pl.BlockSpec(memory_space=pltpu.VMEM)
    tokens, cols = cot.shape
    return pl.pallas_call(
        lambda *refs: product_kernel(offsets, *refs),
        out_shape=[jax.ShapeDtypeStruct((128, cols), dtype) for _ in offsets],
        in_specs=[pl.BlockSpec(memory_space=pltpu.SMEM)] + [vmem] * (2 + len(before)),
        out_specs=[vmem for _ in offsets],
        compiler_params=pltpu.CompilerParams(vmem_limit_bytes=24 * 1024 * 1024),
        cost_estimate=pl.CostEstimate(
            flops=2 * 128 * len(offsets) * tokens * cols,
            bytes_accessed=2 * tokens * (acts.shape[1] + cols),
            transcendentals=0,
        ),
    )(place, acts, cot, *before)


def add(*terms):
    return sum(t.astype(jnp.float32) for t in terms)


def shards(acts, grad_out, inner_weight, first_moment, second_moment, outer_weight, outer_momentum):
    replicas = lax.axis_size(REP)
    high, deep = lax.axis_size("xh"), lax.axis_size("z")
    rows, cols = inner_weight.shape[1:]
    own = rows // replicas
    bf16 = jnp.bfloat16
    place = jnp.stack([lax.axis_index(a) for a in FSDP])

    with jax.named_scope("core_swap"):
        swap = [(0, 1), (1, 0)]
        acts_peer = lax.ppermute(acts[0], "core", swap)
        cot_peer = lax.ppermute(grad_out[0], "core", swap)
    with jax.named_scope("grad_product"):
        mine = product(range(RING), jnp.float32, place, acts[0], grad_out[0])
        farthest = product((RING - 1,), bf16, place, acts_peer, cot_peer, mine[-1])
        blocks = product(range(RING - 1), bf16, place, acts_peer, cot_peer, *mine[:-1])
    with jax.named_scope("grad_ring"):
        hop = [(2 * i, 2 * ((i + 1) % RING)) for i in range(RING)]
        hop += [(2 * ((i + 1) % RING) + 1, 2 * i + 1) for i in range(RING)]
        running = farthest[0]
        for block in blocks[:0:-1]:
            running = add(block, lax.ppermute(running, ("y", "core"), hop)).astype(bf16)
        running = lax.ppermute(running, ("y", "core"), hop)
    with jax.named_scope("grad_pair"):
        other = add(blocks[0][rows:], running[rows:]).astype(bf16)
        other = lax.ppermute(other, "xl", [(0, 1), (1, 0)])
        grad = add(blocks[0][:rows], running[:rows], other)

    with jax.named_scope("adamw"):
        first = 0.9 * first_moment[0] + 0.1 * grad
        second = 0.95 * second_moment[0] + 0.05 * grad * grad
        first_hat = first / (1.0 - 0.9**INNER_STEP)
        second_hat = second / (1.0 - 0.95**INNER_STEP)
        inner_new = inner_weight[0] * (1.0 - 0.0004 * 0.1) - 0.0004 * first_hat / (
            jnp.sqrt(second_hat) + 1e-08
        )
        inner_new = lax.optimization_barrier(inner_new)
    with jax.named_scope("replica_sum"):
        pieces = inner_new.reshape(high, deep, own, cols).transpose(1, 0, 2, 3)
        pieces = lax.all_to_all(pieces.reshape(deep, high * own, cols), "z", 0, 0, tiled=True)
        term = (-0.33 * outer_weight - 0.567 * outer_momentum) * (replicas / OUTER_GAIN)
        mine_here = (jnp.arange(high) == lax.axis_index("xh")).reshape(high, 1, 1)
        total = jnp.sum(pieces, axis=0) + jnp.where(mine_here, term, 0.0).reshape(high * own, cols)
        step = 1
        while step < high:
            total = total + lax.ppermute(total, "xh", [(i, i ^ step) for i in range(high)])
            step *= 2
    with jax.named_scope("row_gather"):
        new = (total * (OUTER_GAIN / replicas)).astype(bf16)
        copies = jnp.broadcast_to(new, (deep,) + new.shape)
        weight_next = lax.all_to_all(copies, "z", 0, 0, tiled=True)
        weight_next = weight_next.reshape(deep, high, own, cols).transpose(1, 0, 2, 3).reshape(rows, cols)
    with jax.named_scope("outer_step"):
        here = jnp.sum(jnp.where(mine_here, total.reshape(high, own, cols), 0.0), axis=0)
        pseudo = outer_weight - (here - term) / replicas
        momentum_next = 0.9 * outer_momentum + pseudo
        outer_next = outer_weight - 0.7 * (pseudo + 0.9 * momentum_next)
    return (outer_next, momentum_next, weight_next)


def solution(mesh, sizes=SIZES):
    grid = Mesh(mesh.devices.reshape(sizes), AXES)
    split = P(REP, FSDP, None)
    outer = P(FSDP + REP, None)
    return jax.shard_map(
        shards,
        mesh=grid,
        in_specs=(split, split, split, split, split, outer, outer),
        out_specs=(outer, outer, P(FSDP, None)),
        check_vma=False,
    )
```

```python
import jax
import jax.numpy as jnp
from jax import lax
from jax.experimental import pallas as pl
from jax.experimental.pallas import tpu as pltpu
from jax.sharding import Mesh, PartitionSpec as P

INNER_STEP = 500
AXES = ("xh", "z", "xl", "y", "core")
SIZES = (4, 8, 2, 8, 2)
REP = ("xh", "z")
FSDP = ("xl", "y", "core")
RING = 8


def product_kernel(offsets, place, acts, cot, *refs):
    xl, y, core = place[0], place[1], place[2]
    before, (near, far) = refs[:-2], refs[-2:]
    lane = lax.broadcasted_iota(jnp.int32, (1, 128), 1)
    own_side = (lane < 64) == (core == 0)

    def columns(target):
        def block(side):
            start = pl.multiple_of((side * RING + target) * 128, 128)
            return acts[:, pl.ds(start, 128)].astype(jnp.float32)

        own, other = block(xl), block(1 - xl)
        still = jnp.where(core == 0, own, other)
        moved = pltpu.roll(jnp.where(core == 0, other, own), 64, 1)
        return jnp.where(own_side, still, moved).astype(jnp.bfloat16)

    for i, offset in enumerate(offsets):
        total = lax.dot_general(
            columns(lax.rem(y + offset, RING)), cot[...], (((0,), (0,)), ((), ())),
            preferred_element_type=jnp.float32,
        )
        for out, part, part_before in zip((near, far), (total[:64], total[64:]), before or (None, None)):
            if before:
                part = part + part_before[i]
            out[i] = part.astype(out.dtype)


def product(offsets, dtype, place, acts, cot, *before):
    vmem = pl.BlockSpec(memory_space=pltpu.VMEM)
    tokens, cols = cot.shape
    return pl.pallas_call(
        lambda *refs: product_kernel(offsets, *refs),
        out_shape=[jax.ShapeDtypeStruct((len(offsets), 64, cols), dtype)] * 2,
        in_specs=[pl.BlockSpec(memory_space=pltpu.SMEM)] + [vmem] * (2 + len(before)),
        out_specs=[vmem] * 2,
        compiler_params=pltpu.CompilerParams(vmem_limit_bytes=24 * 1024 * 1024),
        cost_estimate=pl.CostEstimate(
            flops=2 * 128 * len(offsets) * tokens * cols,
            bytes_accessed=2 * tokens * (acts.shape[1] + cols),
            transcendentals=0,
        ),
    )(place, acts, cot, *before)


def add(*terms):
    return sum(t.astype(jnp.float32) for t in terms)


def shards(acts, grad_out, inner_weight, first_moment, second_moment, outer_weight, outer_momentum):
    replicas = lax.axis_size(REP)
    rows, cols = inner_weight.shape[1:]
    own = rows // replicas
    bf16 = jnp.bfloat16
    place = jnp.stack([lax.axis_index(a) for a in FSDP])

    swap = [(0, 1), (1, 0)]
    ring = [(i, (i + 1) % RING) for i in range(RING)]
    back = [(j, i) for i, j in ring]
    with jax.named_scope("core_swap"):
        acts_peer = lax.ppermute(acts[0], "core", swap)
        cot_peer = lax.ppermute(grad_out[0], "core", swap)
    with jax.named_scope("grad_product"):
        early, late = (4, 3, 5), (2, 6, 1, 7, 0)
        mine_early = product(early, jnp.float32, place, acts[0], grad_out[0])
        mine_late = product(late, jnp.float32, place, acts[0], grad_out[0])
        near, far = product(early, bf16, place, acts_peer, cot_peer, *mine_early)
        near_late, far_late = product(late, bf16, place, acts_peer, cot_peer, *mine_late)
    with jax.named_scope("grad_ring"):
        far_late = lax.ppermute(far_late, "xl", swap)
        up = lax.ppermute(near[0], "y", ring)
        down = lax.ppermute(far[0], "y", back)
        up = jnp.concatenate([add(near[1], up).astype(bf16), far[1]])
        down = jnp.concatenate([near[2], add(far[2], down).astype(bf16)])
        up = lax.ppermute(up, "y", ring)
        down = lax.ppermute(down, "y", back)
        up_far = lax.ppermute(up[rows:], "xl", swap)
        down_far = lax.ppermute(down[rows:], "xl", swap)
        up = add(up[:rows], up_far, near_late[0], far_late[0]).astype(bf16)
        down = add(down[:rows], down_far, near_late[1], far_late[1]).astype(bf16)
        up = lax.ppermute(up, "y", ring)
        down = lax.ppermute(down, "y", back)
        up = add(up, near_late[2], far_late[2]).astype(bf16)
        down = add(down, near_late[3], far_late[3]).astype(bf16)
        up = lax.ppermute(up, "y", ring)
        down = lax.ppermute(down, "y", back)
        grad = add(up, down, near_late[4], far_late[4])

    with jax.named_scope("adamw"):
        first = 0.9 * first_moment[0] + 0.1 * grad
        second = 0.95 * second_moment[0] + 0.05 * grad * grad
        first_hat = first / (1.0 - 0.9**INNER_STEP)
        second_hat = second / (1.0 - 0.95**INNER_STEP)
        inner_new = inner_weight[0] * (1.0 - 0.0004 * 0.1) - 0.0004 * first_hat / (
            jnp.sqrt(second_hat) + 1e-08
        )
        inner_new = lax.optimization_barrier(inner_new)
    with jax.named_scope("replica_sum"):
        pieces = lax.all_to_all(inner_new.reshape(replicas, own, cols), REP, 0, 0, tiled=True)
        summed = jnp.sum(pieces, axis=0)
    with jax.named_scope("outer_step"):
        pseudo = outer_weight - summed / replicas
        momentum_next = 0.9 * outer_momentum + pseudo
        outer_next = outer_weight - 0.7 * (pseudo + 0.9 * momentum_next)
    with jax.named_scope("row_gather"):
        new = outer_next.astype(bf16).reshape(1, own * cols // 128, 128)
        copies = jnp.broadcast_to(new, (replicas,) + new.shape[1:])
        weight_next = lax.all_to_all(copies, REP, 0, 0, tiled=True).reshape(rows, cols)
    return (outer_next, momentum_next, weight_next)


def solution(mesh, sizes=SIZES):
    grid = Mesh(mesh.devices.reshape(sizes), AXES)
    split = P(REP, FSDP, None)
    outer = P(FSDP + REP, None)
    return jax.shard_map(
        shards,
        mesh=grid,
        in_specs=(split, split, split, split, split, outer, outer),
        out_specs=(outer, outer, P(FSDP, None)),
        check_vma=False,
    )
```

```python
import jax
import jax.numpy as jnp
from jax import lax
from jax.experimental import pallas as pl
from jax.experimental.pallas import tpu as pltpu
from jax.sharding import Mesh, PartitionSpec as P

INNER_STEP = 500
AXES = ("xh", "z", "xl", "y", "core")
SIZES = (4, 8, 2, 8, 2)
REP = ("xh", "z")
FSDP = ("xl", "y", "core")
RING = 8


def product_kernel(steps, pairs, place, *refs):
    xl, y, core = place[0], place[1], place[2]
    before, outs = refs[2 * pairs : -len(steps)], refs[-len(steps) :]
    lane = lax.broadcasted_iota(jnp.int32, (1, 128), 1)

    for i, step in enumerate(steps):
        to_core = core if step % 2 else 1 - core
        ahead = RING - 1 - step
        target = lax.rem(y + jnp.where(to_core == 1, ahead, RING - ahead), RING)
        own_side = (lane < 64) == (to_core == 0)

        def columns(ref):
            def block(side):
                start = pl.multiple_of((side * RING + target) * 128, 128)
                return ref[:, pl.ds(start, 128)].astype(jnp.float32)

            near, far = block(xl), block(1 - xl)
            still = jnp.where(to_core == 0, near, far)
            moved = pltpu.roll(jnp.where(to_core == 0, far, near), 64, 1)
            return jnp.where(own_side, still, moved).astype(jnp.bfloat16)

        def times(lhs, rhs):
            return lax.dot_general(lhs, rhs, (((0,), (0,)), ((), ())), preferred_element_type=jnp.float32)

        total = sum(times(columns(refs[2 * k]), refs[2 * k + 1][...]) for k in range(pairs))
        if before:
            total = total + before[i][...]
        outs[i][...] = total.astype(outs[i].dtype)


def product(steps, dtype, place, pairs, before=()):
    vmem = pl.BlockSpec(memory_space=pltpu.VMEM)
    operands = [x for pair in pairs for x in pair] + list(before)
    tokens, cols = pairs[0][1].shape
    return pl.pallas_call(
        lambda *refs: product_kernel(steps, len(pairs), *refs),
        out_shape=[jax.ShapeDtypeStruct((128, cols), dtype) for _ in steps],
        in_specs=[pl.BlockSpec(memory_space=pltpu.SMEM)] + [vmem] * len(operands),
        out_specs=[vmem for _ in steps],
        compiler_params=pltpu.CompilerParams(vmem_limit_bytes=24 * 1024 * 1024),
        cost_estimate=pl.CostEstimate(
            flops=2 * 128 * len(steps) * len(pairs) * tokens * cols,
            bytes_accessed=2 * len(pairs) * tokens * (pairs[0][0].shape[1] + cols),
            transcendentals=0,
        ),
    )(place, *operands)


def add(*terms):
    return sum(t.astype(jnp.float32) for t in terms)


def shards(acts, grad_out, inner_weight, first_moment, second_moment, outer_weight, outer_momentum):
    replicas = lax.axis_size(REP)
    rows, cols = inner_weight.shape[1:]
    own = rows // replicas
    bf16 = jnp.bfloat16
    place = jnp.stack([lax.axis_index(a) for a in FSDP])

    swap = [(0, 1), (1, 0)]
    with jax.named_scope("core_swap"):
        acts_peer = lax.ppermute(acts[0], "core", swap)
        cot_peer = lax.ppermute(grad_out[0], "core", swap)
    with jax.named_scope("grad_product"):
        here, peer = (acts[0], grad_out[0]), (acts_peer, cot_peer)
        first_here = product((0,), jnp.float32, place, [here])
        blocks = product((0,), bf16, place, [peer], first_here)
        blocks = [*blocks, *product((1, 2), bf16, place, [here, peer])]
        blocks = [*blocks, *product((3, 4, 5, 6, 7), bf16, place, [here, peer])]
    with jax.named_scope("grad_ring"):
        links = []
        for core in range(2):
            ends = [(2 * y + core, 2 * ((y + 1) % RING) + 1 - core) for y in range(RING)]
            links.append(ends + [(b, a) for a, b in ends])
        running = blocks[0]
        for step in range(1, RING - 1):
            running = add(blocks[step], lax.ppermute(running, ("y", "core"), links[(step - 1) % 2])).astype(bf16)
        running = lax.ppermute(running, ("y", "core"), links[(RING - 2) % 2])
    with jax.named_scope("grad_pair"):
        other = add(blocks[-1][rows:], running[rows:]).astype(bf16)
        other = lax.ppermute(other, "xl", swap)
        grad = add(blocks[-1][:rows], running[:rows], other)

    with jax.named_scope("adamw"):
        first = 0.9 * first_moment[0] + 0.1 * grad
        second = 0.95 * second_moment[0] + 0.05 * grad * grad
        first_hat = first / (1.0 - 0.9**INNER_STEP)
        second_hat = second / (1.0 - 0.95**INNER_STEP)
        inner_new = inner_weight[0] * (1.0 - 0.0004 * 0.1) - 0.0004 * first_hat / (
            jnp.sqrt(second_hat) + 1e-08
        )
        inner_new = lax.optimization_barrier(inner_new)
    with jax.named_scope("replica_sum"):
        pieces = lax.all_to_all(inner_new.reshape(replicas, own, cols), REP, 0, 0, tiled=True)
        summed = jnp.sum(pieces, axis=0)
    with jax.named_scope("outer_step"):
        pseudo = outer_weight - summed / replicas
        momentum_next = 0.9 * outer_momentum + pseudo
        outer_next = outer_weight - 0.7 * (pseudo + 0.9 * momentum_next)
    with jax.named_scope("row_gather"):
        new = outer_next.astype(bf16).reshape(1, own * cols // 128, 128)
        copies = jnp.broadcast_to(new, (replicas,) + new.shape[1:])
        weight_next = lax.all_to_all(copies, REP, 0, 0, tiled=True).reshape(rows, cols)
    return (outer_next, momentum_next, weight_next)


def solution(mesh, sizes=SIZES):
    grid = Mesh(mesh.devices.reshape(sizes), AXES)
    split = P(REP, FSDP, None)
    outer = P(FSDP + REP, None)
    return jax.shard_map(
        shards,
        mesh=grid,
        in_specs=(split, split, split, split, split, outer, outer),
        out_specs=(outer, outer, P(FSDP, None)),
        check_vma=False,
    )
```

```python
import jax
import jax.numpy as jnp
from jax import lax
from jax.experimental import pallas as pl
from jax.experimental.pallas import tpu as pltpu
from jax.sharding import Mesh, PartitionSpec as P

INNER_STEP = 500
AXES = ("xh", "z", "xl", "y", "core")
SIZES = (4, 8, 2, 8, 2)
REP = ("xh", "z")
FSDP = ("xl", "y", "core")
RING = 8


def product_kernel(offsets, pairs, place, *refs):
    xl, y, core = place[0], place[1], place[2]
    before, outs = refs[2 * pairs : -len(offsets)], refs[-len(offsets) :]
    lane = lax.broadcasted_iota(jnp.int32, (1, 128), 1)

    own_side = (lane < 64) == (core == 0)
    for i, offset in enumerate(offsets):
        target = lax.rem(y + RING + jnp.where(core == 0, offset, -offset), RING)

        def columns(ref):
            def block(side):
                start = pl.multiple_of((side * RING + target) * 128, 128)
                return ref[:, pl.ds(start, 128)].astype(jnp.float32)

            near, far = block(xl), block(1 - xl)
            still = jnp.where(core == 0, near, far)
            moved = pltpu.roll(jnp.where(core == 0, far, near), 64, 1)
            return jnp.where(own_side, still, moved).astype(jnp.bfloat16)

        def times(lhs, rhs):
            return lax.dot_general(lhs, rhs, (((0,), (0,)), ((), ())), preferred_element_type=jnp.float32)

        total = sum(times(columns(refs[2 * k]), refs[2 * k + 1][...]) for k in range(pairs))
        if before:
            total = total + before[i][...]
        outs[i][...] = total.astype(outs[i].dtype)


def product(offsets, dtype, place, pairs, before=()):
    vmem = pl.BlockSpec(memory_space=pltpu.VMEM)
    operands = [x for pair in pairs for x in pair] + list(before)
    tokens, cols = pairs[0][1].shape
    return pl.pallas_call(
        lambda *refs: product_kernel(offsets, len(pairs), *refs),
        out_shape=[jax.ShapeDtypeStruct((128, cols), dtype) for _ in offsets],
        in_specs=[pl.BlockSpec(memory_space=pltpu.SMEM)] + [vmem] * len(operands),
        out_specs=[vmem for _ in offsets],
        compiler_params=pltpu.CompilerParams(vmem_limit_bytes=24 * 1024 * 1024),
        cost_estimate=pl.CostEstimate(
            flops=2 * 128 * len(offsets) * len(pairs) * tokens * cols,
            bytes_accessed=2 * len(pairs) * tokens * (pairs[0][0].shape[1] + cols),
            transcendentals=0,
        ),
    )(place, *operands)


def add(*terms):
    return sum(t.astype(jnp.float32) for t in terms)


def shards(acts, grad_out, inner_weight, first_moment, second_moment, outer_weight, outer_momentum):
    replicas = lax.axis_size(REP)
    rows, cols = inner_weight.shape[1:]
    own = rows // replicas
    bf16 = jnp.bfloat16
    place = jnp.stack([lax.axis_index(a) for a in FSDP])

    swap = [(0, 1), (1, 0)]
    with jax.named_scope("core_swap"):
        acts_peer = lax.ppermute(acts[0], "core", swap)
        cot_peer = lax.ppermute(grad_out[0], "core", swap)
    with jax.named_scope("grad_product"):
        here, peer = (acts[0], grad_out[0]), (acts_peer, cot_peer)
        early = product((-3, 4, 3), bf16, place, [peer], product((-3, 4, 3), jnp.float32, place, [here]))
        late = product((-2, 2, 1, -1, 0), bf16, place, [here, peer])
    with jax.named_scope("grad_ring"):

        def hop(block, k):
            ends = [(2 * y, 2 * ((y + k) % RING)) for y in range(RING)]
            ends += [(2 * y + 1, 2 * ((y - k) % RING) + 1) for y in range(RING)]
            return lax.ppermute(block, ("y", "core"), ends)

        back_3, four, ahead_3 = hop(early[0], -1), hop(early[1], 2), hop(early[2], 1)
        back_2 = hop(add(late[0], back_3).astype(bf16), -2)
        ahead_2 = hop(add(late[1], four, ahead_3).astype(bf16), 2)
        terms = (late[4], back_2, ahead_2, hop(late[2], 1), hop(late[3], -1))
    with jax.named_scope("grad_pair"):
        other = lax.ppermute(add(*(t[rows:] for t in terms)).astype(bf16), "xl", swap)
        grad = add(other, *(t[:rows] for t in terms))

    with jax.named_scope("adamw"):
        first = 0.9 * first_moment[0] + 0.1 * grad
        second = 0.95 * second_moment[0] + 0.05 * grad * grad
        first_hat = first / (1.0 - 0.9**INNER_STEP)
        second_hat = second / (1.0 - 0.95**INNER_STEP)
        inner_new = inner_weight[0] * (1.0 - 0.0004 * 0.1) - 0.0004 * first_hat / (
            jnp.sqrt(second_hat) + 1e-08
        )
        inner_new = lax.optimization_barrier(inner_new)
    with jax.named_scope("replica_sum"):
        pieces = lax.all_to_all(inner_new.reshape(replicas, own, cols), REP, 0, 0, tiled=True)
        summed = jnp.sum(pieces, axis=0)
    with jax.named_scope("outer_step"):
        pseudo = outer_weight - summed / replicas
        momentum_next = 0.9 * outer_momentum + pseudo
        outer_next = outer_weight - 0.7 * (pseudo + 0.9 * momentum_next)
    with jax.named_scope("row_gather"):
        new = outer_next.astype(bf16).reshape(1, own * cols // 128, 128)
        copies = jnp.broadcast_to(new, (replicas,) + new.shape[1:])
        weight_next = lax.all_to_all(copies, REP, 0, 0, tiled=True).reshape(rows, cols)
    return (outer_next, momentum_next, weight_next)


def solution(mesh, sizes=SIZES):
    grid = Mesh(mesh.devices.reshape(sizes), AXES)
    split = P(REP, FSDP, None)
    outer = P(FSDP + REP, None)
    return jax.shard_map(
        shards,
        mesh=grid,
        in_specs=(split, split, split, split, split, outer, outer),
        out_specs=(outer, outer, P(FSDP, None)),
        check_vma=False,
    )
```

```python
import jax
import jax.numpy as jnp
from jax import lax
from jax.experimental import pallas as pl
from jax.experimental.pallas import tpu as pltpu
from jax.sharding import Mesh, PartitionSpec as P

INNER_STEP = 500
AXES = ("xh", "z", "xl", "y", "core")
SIZES = (4, 8, 2, 8, 2)
REP = ("xh", "z")
FSDP = ("xl", "y", "core")
RING = 8


def product_kernel(offsets, pairs, place, *refs):
    xl, y, core = place[0], place[1], place[2]
    before, outs = refs[2 * pairs : -len(offsets)], refs[-len(offsets) :]
    lane = lax.broadcasted_iota(jnp.int32, (1, 128), 1)
    own_side = (lane < 64) == (core == 0)
    for i, offset in enumerate(offsets):
        target = lax.rem(y + RING + jnp.where(core == 0, offset, -offset), RING)

        def columns(ref):
            def block(side):
                start = pl.multiple_of((side * RING + target) * 128, 128)
                return ref[:, pl.ds(start, 128)].astype(jnp.float32)

            near, far = block(xl), block(1 - xl)
            still = jnp.where(core == 0, near, far)
            moved = pltpu.roll(jnp.where(core == 0, far, near), 64, 1)
            return jnp.where(own_side, still, moved).astype(jnp.bfloat16)

        def times(lhs, rhs):
            return lax.dot_general(lhs, rhs, (((0,), (0,)), ((), ())), preferred_element_type=jnp.float32)

        total = sum(times(columns(refs[2 * k]), refs[2 * k + 1][...]) for k in range(pairs))
        if before:
            total = total + before[i][...]
        outs[i][...] = total.astype(outs[i].dtype)


def product(offsets, dtype, place, pairs, before=()):
    vmem = pl.BlockSpec(memory_space=pltpu.VMEM)
    operands = [x for pair in pairs for x in pair] + list(before)
    tokens, cols = pairs[0][1].shape
    return pl.pallas_call(
        lambda *refs: product_kernel(offsets, len(pairs), *refs),
        out_shape=[jax.ShapeDtypeStruct((128, cols), dtype) for _ in offsets],
        in_specs=[pl.BlockSpec(memory_space=pltpu.SMEM)] + [vmem] * len(operands),
        out_specs=[vmem for _ in offsets],
        compiler_params=pltpu.CompilerParams(vmem_limit_bytes=24 * 1024 * 1024),
        cost_estimate=pl.CostEstimate(
            flops=2 * 128 * len(offsets) * len(pairs) * tokens * cols,
            bytes_accessed=2 * len(pairs) * tokens * (pairs[0][0].shape[1] + cols),
            transcendentals=0,
        ),
    )(place, *operands)


def add(*terms):
    return sum(t.astype(jnp.float32) for t in terms)


def shards(acts, grad_out, inner_weight, first_moment, second_moment, outer_weight, outer_momentum):
    replicas = lax.axis_size(REP)
    rows, cols = inner_weight.shape[1:]
    own = rows // replicas
    bf16 = jnp.bfloat16
    place = jnp.stack([lax.axis_index(a) for a in FSDP])

    swap = [(0, 1), (1, 0)]
    with jax.named_scope("core_swap"):
        acts_peer = lax.ppermute(acts[0], "core", swap)
        cot_peer = lax.ppermute(grad_out[0], "core", swap)
    with jax.named_scope("grad_product"):
        here, peer = (acts[0], grad_out[0]), (acts_peer, cot_peer)
        early = product((-3, 4, 3), bf16, place, [peer], product((-3, 4, 3), jnp.float32, place, [here]))
        late = product((-2, 2, 1, -1, 0), bf16, place, [here, peer])
    with jax.named_scope("grad_ring"):

        def hop(block, k):
            ends = [(2 * y, 2 * ((y + k) % RING)) for y in range(RING)]
            ends += [(2 * y + 1, 2 * ((y - k) % RING) + 1) for y in range(RING)]
            return lax.ppermute(block, ("y", "core"), ends)

        back_3, four, ahead_3 = hop(early[0], -1), hop(early[1], 2), hop(early[2], 1)
        back_2 = add(late[0], back_3).astype(bf16)
        ahead_2 = add(late[1], four, ahead_3).astype(bf16)
        back_2, ahead_1 = lax.optimization_barrier((back_2, late[2]))
        ahead_2, back_1 = lax.optimization_barrier((ahead_2, late[3]))
        terms = (late[4], hop(back_2, -2), hop(ahead_2, 2), hop(ahead_1, 1), hop(back_1, -1))
    with jax.named_scope("grad_pair"):
        other = add(*(t[rows:] for t in terms)).astype(bf16)
        other, weight = lax.optimization_barrier((other, inner_weight[0].reshape(replicas, own, cols)))
        other = lax.ppermute(other, "xl", swap)
        weight_sum = jnp.sum(lax.all_to_all(weight, REP, 0, 0, tiled=True), axis=0)
        grad = add(other, *(t[:rows] for t in terms))

    with jax.named_scope("adamw"):
        first = 0.9 * first_moment[0] + 0.1 * grad
        second = 0.95 * second_moment[0] + 0.05 * grad * grad
        first_hat = first / (1.0 - 0.9**INNER_STEP)
        second_hat = second / (1.0 - 0.95**INNER_STEP)
        update = (first_hat / (jnp.sqrt(second_hat) + 1e-08)).astype(bf16)
        update = lax.optimization_barrier(update)
    with jax.named_scope("replica_sum"):
        pieces = lax.all_to_all(update.reshape(replicas, own, cols), REP, 0, 0, tiled=True)
        update_sum = jnp.sum(pieces.astype(jnp.float32), axis=0)
        summed = weight_sum * (1.0 - 0.0004 * 0.1) - 0.0004 * update_sum
    with jax.named_scope("outer_step"):
        pseudo = outer_weight - summed / replicas
        momentum_next = 0.9 * outer_momentum + pseudo
        outer_next = outer_weight - 0.7 * (pseudo + 0.9 * momentum_next)
    with jax.named_scope("row_gather"):
        new = outer_next.astype(bf16).reshape(1, own * cols // 128, 128)
        copies = jnp.broadcast_to(new, (replicas,) + new.shape[1:])
        weight_next = lax.all_to_all(copies, REP, 0, 0, tiled=True).reshape(rows, cols)
    return (outer_next, momentum_next, weight_next)


def solution(mesh, sizes=SIZES):
    grid = Mesh(mesh.devices.reshape(sizes), AXES)
    split = P(REP, FSDP, None)
    outer = P(FSDP + REP, None)
    return jax.shard_map(
        shards,
        mesh=grid,
        in_specs=(split, split, split, split, split, outer, outer),
        out_specs=(outer, outer, P(FSDP, None)),
        check_vma=False,
    )
```

```python
import jax
import jax.numpy as jnp
from jax import lax
from jax.experimental import pallas as pl
from jax.experimental.pallas import tpu as pltpu
from jax.sharding import Mesh, PartitionSpec as P

INNER_STEP = 500
AXES = ("xh", "z", "xl", "y", "core")
SIZES = (4, 8, 2, 8, 2)
REP = ("xh", "z")
FSDP = ("xl", "y", "core")
RING = 8


def product_kernel(offsets, sources, wide, place, *refs):
    xl, y, core = place[0], place[1], place[2]
    before, outs = refs[sources : -len(offsets)], refs[-len(offsets) :]
    lane = lax.broadcasted_iota(jnp.int32, (1, 128), 1)
    own_side = (lane < 64) == (core == 0)
    for i, offset in enumerate(offsets):
        target = lax.rem(y + RING + jnp.where(core == 0, offset, -offset), RING)

        def columns(ref):
            def block(side):
                start = pl.multiple_of((side * RING + target) * 128, 128)
                return ref[:, pl.ds(start, 128)].astype(jnp.float32)

            near, far = block(xl), block(1 - xl)
            still = jnp.where(core == 0, near, far)
            moved = pltpu.roll(jnp.where(core == 0, far, near), 64, 1)
            return jnp.where(own_side, still, moved).astype(jnp.bfloat16)

        def times(lhs, rhs):
            return lax.dot_general(lhs, rhs, (((0,), (0,)), ((), ())), preferred_element_type=jnp.float32)

        total = sum(times(columns(ref), ref[:, wide:]) for ref in refs[:sources])
        if before:
            total = total + before[i][...]
        outs[i][...] = total.astype(outs[i].dtype)


def product(offsets, dtype, place, sources, cols, before=()):
    vmem = pl.BlockSpec(memory_space=pltpu.VMEM)
    operands = [*sources, *before]
    tokens, wide = sources[0].shape
    return pl.pallas_call(
        lambda *refs: product_kernel(offsets, len(sources), wide - cols, *refs),
        out_shape=[jax.ShapeDtypeStruct((128, cols), dtype) for _ in offsets],
        in_specs=[pl.BlockSpec(memory_space=pltpu.SMEM)] + [vmem] * len(operands),
        out_specs=[vmem for _ in offsets],
        compiler_params=pltpu.CompilerParams(vmem_limit_bytes=24 * 1024 * 1024),
        cost_estimate=pl.CostEstimate(
            flops=2 * 128 * len(offsets) * len(sources) * tokens * cols,
            bytes_accessed=2 * len(sources) * tokens * wide,
            transcendentals=0,
        ),
    )(place, *operands)


def add(*terms):
    return sum(t.astype(jnp.float32) for t in terms)


def shards(acts, grad_out, inner_weight, first_moment, second_moment, outer_weight, outer_momentum):
    replicas = lax.axis_size(REP)
    rows, cols = inner_weight.shape[1:]
    own = rows // replicas
    bf16 = jnp.bfloat16
    place = jnp.stack([lax.axis_index(a) for a in FSDP])

    swap = [(0, 1), (1, 0)]
    with jax.named_scope("core_swap"):
        here = jnp.concatenate([acts[0], grad_out[0]], axis=1)
        peer = lax.ppermute(here, "core", swap)
    with jax.named_scope("grad_product"):
        mine = product((-3, 4, 3), jnp.float32, place, [here], cols)
        early = product((-3, 4, 3), bf16, place, [peer], cols, mine)
        late = product((-2, 2, 1, -1, 0), bf16, place, [here, peer], cols)
    with jax.named_scope("grad_ring"):

        def hop(block, k):
            ends = [(2 * y, 2 * ((y + k) % RING)) for y in range(RING)]
            ends += [(2 * y + 1, 2 * ((y - k) % RING) + 1) for y in range(RING)]
            return lax.ppermute(block, ("y", "core"), ends)

        back_3, four, ahead_3 = hop(early[0], -1), hop(early[1], 2), hop(early[2], 1)
        back_2 = hop(add(late[0], back_3).astype(bf16), -1)
        ahead_2 = hop(add(late[1], four, ahead_3).astype(bf16), 1)
        ahead_1 = hop(add(late[2], ahead_2).astype(bf16), 1)
        back_1 = hop(add(late[3], back_2).astype(bf16), -1)
        terms = (late[4], ahead_1, back_1)
    with jax.named_scope("grad_pair"):
        other = lax.ppermute(add(*(t[rows:] for t in terms)).astype(bf16), "xl", swap)
        grad = add(other, *(t[:rows] for t in terms))

    with jax.named_scope("adamw"):
        first = 0.9 * first_moment[0] + 0.1 * grad
        second = 0.95 * second_moment[0] + 0.05 * grad * grad
        first_hat = first / (1.0 - 0.9**INNER_STEP)
        second_hat = second / (1.0 - 0.95**INNER_STEP)
        inner_new = inner_weight[0] * (1.0 - 0.0004 * 0.1) - 0.0004 * first_hat / (
            jnp.sqrt(second_hat) + 1e-08
        )
        inner_new = lax.optimization_barrier(inner_new)
    with jax.named_scope("replica_sum"):
        pieces = lax.all_to_all(inner_new.reshape(replicas, own, cols), REP, 0, 0, tiled=True)
        summed = jnp.sum(pieces, axis=0)
    with jax.named_scope("outer_step"):
        pseudo = outer_weight - summed / replicas
        momentum_next = 0.9 * outer_momentum + pseudo
        outer_next = outer_weight - 0.7 * (pseudo + 0.9 * momentum_next)
    with jax.named_scope("row_gather"):
        new = outer_next.astype(bf16).reshape(1, own * cols // 128, 128)
        copies = jnp.broadcast_to(new, (replicas,) + new.shape[1:])
        weight_next = lax.all_to_all(copies, REP, 0, 0, tiled=True).reshape(rows, cols)
    return (outer_next, momentum_next, weight_next)


def solution(mesh, sizes=SIZES):
    grid = Mesh(mesh.devices.reshape(sizes), AXES)
    split = P(REP, FSDP, None)
    outer = P(FSDP + REP, None)
    return jax.shard_map(
        shards,
        mesh=grid,
        in_specs=(split, split, split, split, split, outer, outer),
        out_specs=(outer, outer, P(FSDP, None)),
        check_vma=False,
    )
```

```python
import jax
import jax.numpy as jnp
from jax import lax
from jax.experimental import pallas as pl
from jax.experimental.pallas import tpu as pltpu
from jax.sharding import Mesh, PartitionSpec as P

INNER_STEP = 500
AXES = ("xh", "z", "xl", "y", "core")
SIZES = (4, 8, 2, 8, 2)
REP = ("xh", "z")
FSDP = ("xl", "y", "core")
RING = 8


def product_kernel(offsets, sources, wide, place, *refs):
    xl, y, core = place[0], place[1], place[2]
    before, outs = refs[sources : -len(offsets)], refs[-len(offsets) :]
    lane = lax.broadcasted_iota(jnp.int32, (1, 128), 1)
    own_side = (lane < 64) == (core == 0)
    for i, offset in enumerate(offsets):
        target = lax.rem(y + RING + jnp.where(core == 0, offset, -offset), RING)

        def columns(ref):
            def block(side):
                start = pl.multiple_of((side * RING + target) * 128, 128)
                return ref[:, pl.ds(start, 128)].astype(jnp.float32)

            near, far = block(xl), block(1 - xl)
            still = jnp.where(core == 0, near, far)
            moved = pltpu.roll(jnp.where(core == 0, far, near), 64, 1)
            return jnp.where(own_side, still, moved).astype(jnp.bfloat16)

        def times(lhs, rhs):
            return lax.dot_general(lhs, rhs, (((0,), (0,)), ((), ())), preferred_element_type=jnp.float32)

        total = sum(times(columns(ref), ref[:, wide:]) for ref in refs[:sources])
        if before:
            total = total + before[i][...]
        outs[i][...] = total.astype(outs[i].dtype)


def product(offsets, dtype, place, sources, cols, before=()):
    vmem = pl.BlockSpec(memory_space=pltpu.VMEM)
    operands = [*sources, *before]
    tokens, wide = sources[0].shape
    return pl.pallas_call(
        lambda *refs: product_kernel(offsets, len(sources), wide - cols, *refs),
        out_shape=[jax.ShapeDtypeStruct((128, cols), dtype) for _ in offsets],
        in_specs=[pl.BlockSpec(memory_space=pltpu.SMEM)] + [vmem] * len(operands),
        out_specs=[vmem for _ in offsets],
        compiler_params=pltpu.CompilerParams(vmem_limit_bytes=24 * 1024 * 1024),
        cost_estimate=pl.CostEstimate(
            flops=2 * 128 * len(offsets) * len(sources) * tokens * cols,
            bytes_accessed=2 * len(sources) * tokens * wide,
            transcendentals=0,
        ),
    )(place, *operands)


def add(*terms):
    return sum(t.astype(jnp.float32) for t in terms)


def shards(acts, grad_out, inner_weight, first_moment, second_moment, outer_weight, outer_momentum):
    replicas = lax.axis_size(REP)
    rows, cols = inner_weight.shape[1:]
    own = rows // replicas
    bf16 = jnp.bfloat16
    place = jnp.stack([lax.axis_index(a) for a in FSDP])

    swap = [(0, 1), (1, 0)]
    with jax.named_scope("core_swap"):
        here = jnp.concatenate([acts[0], grad_out[0]], axis=1)
        peer = lax.ppermute(here, "core", swap)
    with jax.named_scope("grad_product"):
        mine = product((-3, 4, 3), jnp.float32, place, [here], cols)
        early = product((-3, 4, 3), bf16, place, [peer], cols, mine)
        late = product((-2, 2, 1, -1, 0), bf16, place, [here, peer], cols)
    with jax.named_scope("grad_ring"):
        def hop(block, k):
            ends = [(2 * y, 2 * ((y + k) % RING)) for y in range(RING)]
            ends += [(2 * y + 1, 2 * ((y - k) % RING) + 1) for y in range(RING)]
            return lax.ppermute(block, ("y", "core"), ends)

        back_3, four, ahead_3 = hop(early[0], -1), hop(early[1], 2), hop(early[2], 1)
        ahead_1 = hop(late[2], 1)
        back_2 = hop(add(late[0], back_3).astype(bf16), -1)
        ahead_2 = hop(add(late[1], four, ahead_3).astype(bf16), 2)
        back_1 = hop(add(late[3], back_2).astype(bf16), -1)
        terms = (late[4], ahead_1, ahead_2, back_1)
    with jax.named_scope("grad_pair"):
        other = lax.ppermute(add(*(t[rows:] for t in terms)).astype(bf16), "xl", swap)
        grad = add(other, *(t[:rows] for t in terms))

    with jax.named_scope("adamw"):
        first = 0.9 * first_moment[0] + 0.1 * grad
        second = 0.95 * second_moment[0] + 0.05 * grad * grad
        first_hat = first / (1.0 - 0.9**INNER_STEP)
        second_hat = second / (1.0 - 0.95**INNER_STEP)
        inner_new = inner_weight[0] * (1.0 - 0.0004 * 0.1) - 0.0004 * first_hat / (
            jnp.sqrt(second_hat) + 1e-08
        )
        inner_new = lax.optimization_barrier(inner_new)
    with jax.named_scope("replica_sum"):
        pieces = lax.all_to_all(inner_new.reshape(replicas, own, cols), REP, 0, 0, tiled=True)
        summed = jnp.sum(pieces, axis=0)
    with jax.named_scope("outer_step"):
        pseudo = outer_weight - summed / replicas
        momentum_next = 0.9 * outer_momentum + pseudo
        outer_next = outer_weight - 0.7 * (pseudo + 0.9 * momentum_next)
    with jax.named_scope("row_gather"):
        new = outer_next.astype(bf16).reshape(1, own * cols // 128, 128)
        copies = jnp.broadcast_to(new, (replicas,) + new.shape[1:])
        weight_next = lax.all_to_all(copies, REP, 0, 0, tiled=True).reshape(rows, cols)
    return (outer_next, momentum_next, weight_next)


def solution(mesh, sizes=SIZES):
    grid = Mesh(mesh.devices.reshape(sizes), AXES)
    split = P(REP, FSDP, None)
    outer = P(FSDP + REP, None)
    return jax.shard_map(
        shards,
        mesh=grid,
        in_specs=(split, split, split, split, split, outer, outer),
        out_specs=(outer, outer, P(FSDP, None)),
        check_vma=False,
    )
```

```python
import jax
import jax.numpy as jnp
from jax import lax
from jax.experimental import pallas as pl
from jax.experimental.pallas import tpu as pltpu
from jax.sharding import Mesh, PartitionSpec as P

INNER_STEP = 500
AXES = ("xh", "z", "xl", "y", "core")
SIZES = (4, 8, 2, 8, 2)
REP = ("xh", "z")
FSDP = ("xl", "y", "core")
RING = 8


def product_kernel(offsets, sources, wide, place, *refs):
    xl, y, core = place[0], place[1], place[2]
    before, outs = refs[sources : -len(offsets)], refs[-len(offsets) :]
    lane = lax.broadcasted_iota(jnp.int32, (1, 128), 1)
    own_side = (lane < 64) == (core == 0)
    for i, offset in enumerate(offsets):
        target = lax.rem(y + RING + jnp.where(core == 0, offset, -offset), RING)

        def columns(ref):
            def block(side):
                start = pl.multiple_of((side * RING + target) * 128, 128)
                return ref[:, pl.ds(start, 128)].astype(jnp.float32)

            near, far = block(xl), block(1 - xl)
            still = jnp.where(core == 0, near, far)
            moved = pltpu.roll(jnp.where(core == 0, far, near), 64, 1)
            return jnp.where(own_side, still, moved).astype(jnp.bfloat16)

        def times(lhs, rhs):
            return lax.dot_general(lhs, rhs, (((0,), (0,)), ((), ())), preferred_element_type=jnp.float32)

        total = sum(times(columns(ref), ref[:, wide:]) for ref in refs[:sources])
        if before:
            total = total + before[i][...]
        outs[i][...] = total.astype(outs[i].dtype)


def product(offsets, dtype, place, sources, cols, before=()):
    vmem = pl.BlockSpec(memory_space=pltpu.VMEM)
    operands = [*sources, *before]
    tokens, wide = sources[0].shape
    return pl.pallas_call(
        lambda *refs: product_kernel(offsets, len(sources), wide - cols, *refs),
        out_shape=[jax.ShapeDtypeStruct((128, cols), dtype) for _ in offsets],
        in_specs=[pl.BlockSpec(memory_space=pltpu.SMEM)] + [vmem] * len(operands),
        out_specs=[vmem for _ in offsets],
        compiler_params=pltpu.CompilerParams(vmem_limit_bytes=24 * 1024 * 1024),
        cost_estimate=pl.CostEstimate(
            flops=2 * 128 * len(offsets) * len(sources) * tokens * cols,
            bytes_accessed=2 * len(sources) * tokens * wide,
            transcendentals=0,
        ),
    )(place, *operands)


def add(*terms):
    return sum(t.astype(jnp.float32) for t in terms)


def shards(acts, grad_out, inner_weight, first_moment, second_moment, outer_weight, outer_momentum):
    replicas = lax.axis_size(REP)
    rows, cols = inner_weight.shape[1:]
    own = rows // replicas
    bf16 = jnp.bfloat16
    place = jnp.stack([lax.axis_index(a) for a in FSDP])

    swap = [(0, 1), (1, 0)]
    with jax.named_scope("core_swap"):
        here = jnp.concatenate([acts[0], grad_out[0]], axis=1)
        peer = lax.ppermute(here, "core", swap)
    with jax.named_scope("grad_product"):
        mine = product((-3, 4, 3), jnp.float32, place, [here], cols)
        early = product((-3, 4, 3), bf16, place, [peer], cols, mine)
        late = product((-2, 2, 1, -1, 0), bf16, place, [here, peer], cols)
    with jax.named_scope("grad_ring"):
        def hop(block, k):
            ends = [(2 * y, 2 * ((y + k) % RING)) for y in range(RING)]
            ends += [(2 * y + 1, 2 * ((y - k) % RING) + 1) for y in range(RING)]
            return lax.ppermute(block, ("y", "core"), ends)

        def across(block, k):
            ends = []
            for xl in range(2):
                ends += [(16 * xl + 2 * y, 16 * (1 - xl) + 2 * ((y + k) % RING)) for y in range(RING)]
                ends += [(16 * xl + 2 * y + 1, 16 * (1 - xl) + 2 * ((y - k) % RING) + 1) for y in range(RING)]
            return lax.ppermute(block, FSDP, ends)

        back_3, four, ahead_3 = hop(early[0], -1), hop(early[1], 2), hop(early[2], 1)
        ahead_1 = hop(late[2], 1)
        back_2 = hop(add(late[0], back_3).astype(bf16), -1)
        ahead_2 = add(late[1], four, ahead_3).astype(bf16)
        back_1 = add(late[3], back_2).astype(bf16)
        ahead_2, ahead_2_far = hop(ahead_2[:rows], 2), across(ahead_2[rows:], 2)
        back_1, back_1_far = hop(back_1[:rows], -1), across(back_1[rows:], -1)
        far = across(add(late[4][rows:], ahead_1[rows:]).astype(bf16), 0)
        grad = add(late[4][:rows], ahead_1[:rows], ahead_2, back_1, ahead_2_far, back_1_far, far)

    with jax.named_scope("adamw"):
        first = 0.9 * first_moment[0] + 0.1 * grad
        second = 0.95 * second_moment[0] + 0.05 * grad * grad
        first_hat = first / (1.0 - 0.9**INNER_STEP)
        second_hat = second / (1.0 - 0.95**INNER_STEP)
        inner_new = inner_weight[0] * (1.0 - 0.0004 * 0.1) - 0.0004 * first_hat / (
            jnp.sqrt(second_hat) + 1e-08
        )
        inner_new = lax.optimization_barrier(inner_new)
    with jax.named_scope("replica_sum"):
        pieces = lax.all_to_all(inner_new.reshape(replicas, own, cols), REP, 0, 0, tiled=True)
        summed = jnp.sum(pieces, axis=0)
    with jax.named_scope("outer_step"):
        pseudo = outer_weight - summed / replicas
        momentum_next = 0.9 * outer_momentum + pseudo
        outer_next = outer_weight - 0.7 * (pseudo + 0.9 * momentum_next)
    with jax.named_scope("row_gather"):
        new = outer_next.astype(bf16).reshape(1, own * cols // 128, 128)
        copies = jnp.broadcast_to(new, (replicas,) + new.shape[1:])
        weight_next = lax.all_to_all(copies, REP, 0, 0, tiled=True).reshape(rows, cols)
    return (outer_next, momentum_next, weight_next)


def solution(mesh, sizes=SIZES):
    grid = Mesh(mesh.devices.reshape(sizes), AXES)
    split = P(REP, FSDP, None)
    outer = P(FSDP + REP, None)
    return jax.shard_map(
        shards,
        mesh=grid,
        in_specs=(split, split, split, split, split, outer, outer),
        out_specs=(outer, outer, P(FSDP, None)),
        check_vma=False,
    )
```
